256 devices in a mesh: row: 32 (over x, y, core), col: 8 (over z).
Axes of the slice: x: 4, y: 4, z: 8, core: 2. Of those that a mesh axis runs over, the one named last changes fastest.
Arguments:
- activations: bfloat16 [32768, 16384], P('row', 'col'), may hold values from -200 to 200
- sketch: bfloat16 [16384, 512], P('col'), may hold values from -0.046875 to 0.046875
Outputs:
- scaled_basis: float32 [32768, 512], P('row')
- coefficients: float32 [512, 16384], P('row', 'col')
The draws below stay inside these ranges and needn't reach their ends.
All inputs are finite; a program needn't handle non-finite values.
Results may differ from the reference program's by a relative error of at most 0.0047.
Values may be sent and summed in bfloat16 or wider, within the bound.
No kernel may reach another device: no remote copies, remote signals or barrier semaphores. Data moves between devices by JAX's collectives and lax.ppermute only.
A program may use at most 64 MiB of HBM per device.

```python
import math
import jax
import jax.numpy as jnp
from jax import lax

D = 16384
K = 512
ROWS = 32768


def draw_activations(key, part):
    key = jax.random.fold_in(key, 11)
    key_base, key_rows, key_cols, key_pick, key_loud = jax.random.split(key, 5)
    scale_rows = jnp.exp(jax.random.uniform(key_rows, (ROWS, 1), jnp.float32, math.log(0.5), math.log(2.0)))
    scale_cols = jnp.exp(jax.random.uniform(key_cols, (1, D), jnp.float32, math.log(0.5), math.log(2.0)))
    picked = jax.random.permutation(key_pick, D) < K
    loudness = jnp.exp(jax.random.uniform(key_loud, (D,), jnp.float32, math.log(4.0), math.log(8.0)))
    channel = jnp.where(picked, loudness, jnp.float32(1.0)).reshape(1, D)
    values = jax.random.truncated_normal(key_base, -6.0, 6.0, (ROWS, D), jnp.float32)
    return (values * scale_rows * scale_cols * channel).astype(jnp.bfloat16)


def block_scale(own_key, shape, cuts, low, high):
    level, own = 1.0, jax.random.fold_in(own_key, 6)
    for axis_at, blocks in cuts:
        draws = jnp.exp(jax.random.uniform(jax.random.fold_in(own, axis_at), (blocks,), jnp.float32, low / len(cuts), high / len(cuts)))
        level = level * jnp.repeat(draws, shape[axis_at] // blocks).reshape([-1 if axis == axis_at else 1 for axis in range(len(shape))])
    return level


def scatter_about(stream_key, shape, width, limit, shards=(), held_as=jnp.bfloat16):
    array = jax.random.normal(stream_key, shape, jnp.float32) * width
    if len(shards) > 0:
        array = block_scale(stream_key, shape, shards, -0.22, 0.18) * array
    return jnp.clip(array, min=-limit, max=limit).astype(held_as)


def setup_inputs(seed: int = 0) -> dict:
    arg_keys = jax.random.split(jax.random.key(seed), 3)
    activations = draw_activations(jax.random.fold_in(arg_keys[2], 71), 0)
    sketch = scatter_about(arg_keys[1], (D, K), D ** -0.5, 0.046875, ((0, 8),))
    return dict(activations=activations, sketch=sketch)


def orthonormal(sampled):
    gram_matrix = jnp.dot(sampled.T.astype(jnp.float32), sampled.astype(jnp.float32), precision=lax.Precision.HIGHEST, preferred_element_type=jnp.float32)
    lower_factor = jnp.linalg.cholesky(gram_matrix)
    return jax.scipy.linalg.solve_triangular(lower_factor, sampled.T, lower=True).T

def reference(activations, sketch):
    sampled = jnp.dot(activations.astype(jnp.float32), sketch.astype(jnp.float32), preferred_element_type=jnp.float32)
    basis_half = orthonormal(sampled).astype(jnp.bfloat16)
    gathered = lax.dot_general(activations.astype(jnp.float32), basis_half.astype(jnp.float32), (((0,), (0,)), ((), ())), preferred_element_type=jnp.float32)
    gathered = gathered.astype(jnp.bfloat16)
    sampled = jnp.dot(activations.astype(jnp.float32), gathered.astype(jnp.float32), preferred_element_type=jnp.float32)
    basis_two = orthonormal(sampled)
    basis_half = basis_two.astype(jnp.bfloat16)
    coefficients = lax.dot_general(basis_half.astype(jnp.float32), activations.astype(jnp.float32), (((0,), (0,)), ((), ())), preferred_element_type=jnp.float32)
    scaled_basis = math.sqrt(ROWS) * basis_two
    return (scaled_basis, coefficients)
```

```python
import math

import jax
import jax.numpy as jnp
from jax import lax
from jax.experimental import pallas as pl
from jax.experimental.pallas import tpu as pltpu
from jax.sharding import PartitionSpec as P

F32 = jnp.float32
BF16 = jnp.bfloat16
HIGHEST = lax.Precision.HIGHEST
BLOCK = 128
PANEL = 8


def reciprocal(value):
    guess = pl.reciprocal(value, approx=True)
    guess = guess * (2.0 - value * guess)
    return guess * (2.0 - value * guess)


def factor_block(tiles):
    lane = lax.broadcasted_iota(jnp.int32, (PANEL, BLOCK), 1)
    sub = lax.broadcasted_iota(jnp.int32, (PANEL, BLOCK), 0)
    tiles = list(tiles)

    def over_lanes(tile, at):
        return jnp.broadcast_to(tile[:, at : at + 1], (PANEL, BLOCK))

    def over_rows(tile, at):
        return jnp.broadcast_to(tile[at : at + 1, :], (PANEL, BLOCK))

    for g in range(len(tiles)):
        first = PANEL * g
        pivot = [over_lanes(tiles[g], first + l) for l in range(PANEL)]
        entry = [[over_rows(pivot[l], m) for l in range(m + 1)] for m in range(PANEL)]
        ratio = [[None] * PANEL for _ in range(PANEL)]
        inverse = [None] * PANEL
        for j in range(PANEL):
            if j % 2 == 0:
                a, b, c = entry[j][j], entry[j + 1][j], entry[j + 1][j + 1]
                inverse[j] = reciprocal(a)
                inverse[j + 1] = a * reciprocal(a * c - b * b)
            for m in range(j + 1, PANEL):
                ratio[j][m] = entry[m][j] * inverse[j]
            for m in range(j + 1, PANEL):
                for l in range(j + 1, m + 1):
                    entry[m][l] = entry[m][l] - entry[m][j] * ratio[j][l]
        inside = (lane >= first) & (lane < first + PANEL)
        start = jnp.where(inside, jnp.where(lane == sub + first, 1.0, 0.0), tiles[g])
        rows = []
        for m in range(PANEL):
            row = over_rows(start, m)
            for l in range(m):
                row = row - ratio[l][m] * rows[l]
            rows.append(row)
        scaled = [rows[m] * inverse[m] for m in range(PANEL)]
        for i in range(g + 1, len(tiles)):
            columns = []
            total = jnp.where(inside, 0.0, tiles[i])
            for m in range(PANEL):
                column = over_lanes(tiles[i], first + m)
                for l in range(m):
                    column = column - ratio[l][m] * columns[l]
                columns.append(column)
                total = total - column * scaled[m]
            tiles[i] = total
        squared, own = inverse[0], rows[0]
        for m in range(1, PANEL):
            squared = jnp.where(sub == m, inverse[m], squared)
            own = jnp.where(sub == m, rows[m], own)
        tiles[g] = own * (squared * lax.rsqrt(squared))
    return tiles


def inverse_factor_kernel(gram_ref, out_ref, work):
    n = gram_ref.shape[0]
    row_at = lax.broadcasted_iota(jnp.int32, (n, n), 0)
    col_at = lax.broadcasted_iota(jnp.int32, (n, n), 1)
    gram = gram_ref[...]
    diagonal = jnp.where(row_at == col_at, gram, 0.0)
    scale_cols = lax.rsqrt(jnp.sum(diagonal, axis=0, keepdims=True))
    scale_rows = lax.rsqrt(jnp.sum(diagonal, axis=1, keepdims=True))
    work[...] = gram * (scale_rows * scale_cols)

    def step(k, carry):
        first = pl.multiple_of(k * BLOCK, BLOCK)
        own = pl.ds(first, BLOCK)
        block = work[own, own]
        tiles = factor_block([block[PANEL * i : PANEL * (i + 1), :] for i in range(BLOCK // PANEL)])
        ri = lax.broadcasted_iota(jnp.int32, (BLOCK, BLOCK), 0)
        ci = lax.broadcasted_iota(jnp.int32, (BLOCK, BLOCK), 1)
        lower_inverse = jnp.where(ci <= ri, jnp.concatenate(tiles, axis=0), 0.0)
        work[own, own] = jnp.where(ci == ri, 1.0, 0.0)
        rows = jnp.dot(lower_inverse, work[own, :], precision=HIGHEST, preferred_element_type=F32)
        cols = lax.broadcasted_iota(jnp.int32, (BLOCK, n), 1)
        upper = jnp.where(cols >= first + BLOCK, rows, 0.0)
        below = lax.broadcasted_iota(jnp.int32, (n, BLOCK), 0) >= first + BLOCK
        work[:, own] = jnp.where(below, 0.0, work[:, own])
        work[...] -= lax.dot_general(
            upper, rows, (((0,), (0,)), ((), ())), precision=HIGHEST, preferred_element_type=F32
        )
        work[own, :] = rows
        return carry

    lax.fori_loop(0, n // BLOCK, step, 0)
    out_ref[...] = jnp.where(col_at <= row_at, work[...], 0.0) * scale_cols


def inverse_factor(gram):
    n = gram.shape[0]
    return pl.pallas_call(
        inverse_factor_kernel,
        out_shape=jax.ShapeDtypeStruct((n, n), F32),
        scratch_shapes=[pltpu.VMEM((n, n), F32)],
        compiler_params=pltpu.CompilerParams(vmem_limit_bytes=16 << 20),
        cost_estimate=pl.CostEstimate(flops=2 * n**3, bytes_accessed=8 * n * n, transcendentals=4 * n),
    )(gram)


def exchange(pieces, axis, groups=None):
    return lax.all_to_all(pieces, axis, 0, 0, tiled=True, axis_index_groups=groups)


def spread(share, axis, count, groups=None):
    copies = lax.optimization_barrier(jnp.broadcast_to(share[None], (count,) + share.shape))
    return exchange(copies, axis, groups)


def swap_cores(array):
    rows = lax.axis_size("row")
    return lax.ppermute(array, "row", [(i, i ^ 1) for i in range(rows)])


def same_core():
    rows = lax.axis_size("row")
    return [list(range(core, rows, 2)) for core in range(2)]


def sum_gram(share):
    rows, cols = lax.axis_size("row"), lax.axis_size("col")
    part = lax.dot_general(
        share, share, (((0,), (0,)), ((), ())), precision=HIGHEST, preferred_element_type=F32
    )
    n = part.shape[0]
    own = jnp.sum(exchange(part.reshape(rows, n // rows, n), "row"), axis=0)
    own = jnp.sum(spread(own, "col", cols), axis=0)
    return spread(own, "row", rows).reshape(n, n)


def sum_rows(partial):
    core = lax.rem(lax.axis_index("row"), 2)
    away = lax.dynamic_index_in_dim(partial, 1 - core, 1, keepdims=False).astype(BF16)
    stay = lax.dynamic_index_in_dim(partial, core, 1, keepdims=False)
    pair = (stay + swap_cores(away).astype(F32)).astype(BF16)
    return jnp.sum(exchange(pair, "row", same_core()).astype(F32), axis=0)


def gather_rows(share):
    chips = lax.axis_size("row") // 2
    core = lax.rem(lax.axis_index("row"), 2)
    mine = spread(share, "row", chips, same_core())
    other = swap_cores(mine)
    first = jnp.where(core == 0, mine, other)
    second = jnp.where(core == 0, other, mine)
    return jnp.stack([first, second], axis=1)


def orthonormal(partial):
    share = lax.psum_scatter(partial, "col", scatter_dimension=0, tiled=True)
    sampled = lax.all_gather(share, "col", axis=0, tiled=True)
    lower_inverse = inverse_factor(sum_gram(share))
    return lax.dot_general(
        sampled, lower_inverse, (((1,), (1,)), ((), ())), precision=HIGHEST, preferred_element_type=F32
    )


def body(activations, sketch):
    rows_dev, cols_dev = activations.shape
    rank = sketch.shape[1]
    row_count = lax.axis_size("row")
    chips = row_count // 2
    contract_rows = (((0,), (0,)), ((), ()))
    basis_half = orthonormal(jnp.dot(activations, sketch, preferred_element_type=F32)).astype(BF16)
    partial_sum = lax.dot_general(activations, basis_half, contract_rows, preferred_element_type=F32)
    own = sum_rows(partial_sum.reshape(chips, 2, cols_dev // row_count, rank)).astype(BF16)
    gathered = gather_rows(own).reshape(cols_dev, rank)
    basis_two = orthonormal(jnp.dot(activations, gathered, preferred_element_type=F32))
    basis_half = basis_two.astype(BF16)
    projected = lax.dot_general(basis_half, activations, contract_rows, preferred_element_type=F32)
    coefficients = sum_rows(projected.reshape(chips, 2, rank // row_count, cols_dev))
    scaled_basis = math.sqrt(rows_dev * row_count) * basis_two
    return (scaled_basis, coefficients)


def solution(mesh):
    in_specs = (P("row", "col"), P("col", None))
    out_specs = (P("row", None), P("row", "col"))
    return jax.shard_map(body, mesh=mesh, in_specs=in_specs, out_specs=out_specs, check_vma=False)
```

```python
import math

import jax
import jax.numpy as jnp
from jax import lax
from jax.experimental import pallas as pl
from jax.experimental.pallas import tpu as pltpu
from jax.sharding import PartitionSpec as P

F32 = jnp.float32
BF16 = jnp.bfloat16
HIGHEST = lax.Precision.HIGHEST
BLOCK = 128
PANEL = 8


def factor_block(tiles):
    lane = lax.broadcasted_iota(jnp.int32, (PANEL, BLOCK), 1)
    sub = lax.broadcasted_iota(jnp.int32, (PANEL, BLOCK), 0)
    tiles = list(tiles)

    def over_lanes(tile, at):
        return jnp.broadcast_to(tile[:, at : at + 1], (PANEL, BLOCK))

    def over_rows(tile, at):
        return jnp.broadcast_to(tile[at : at + 1, :], (PANEL, BLOCK))

    for g in range(len(tiles)):
        first = PANEL * g
        pivot = [over_lanes(tiles[g], first + l) for l in range(PANEL)]
        entry = [[over_rows(pivot[l], m) for l in range(m + 1)] for m in range(PANEL)]
        ratio = [[None] * PANEL for _ in range(PANEL)]
        inverse = [None] * PANEL
        for j in range(PANEL):
            if j % 2 == 0:
                a, b, c = entry[j][j], entry[j + 1][j], entry[j + 1][j + 1]
                inverse[j] = 1.0 / a
                inverse[j + 1] = a * (1.0 / (a * c - b * b))
            for m in range(j + 1, PANEL):
                ratio[j][m] = entry[m][j] * inverse[j]
            for m in range(j + 1, PANEL):
                for l in range(j + 1, m + 1):
                    entry[m][l] = entry[m][l] - entry[m][j] * ratio[j][l]
        inside = (lane >= first) & (lane < first + PANEL)
        start = jnp.where(inside, jnp.where(lane == sub + first, 1.0, 0.0), tiles[g])
        rows = []
        for m in range(PANEL):
            row = over_rows(start, m)
            for l in range(m):
                row = row - ratio[l][m] * rows[l]
            rows.append(row)
        scaled = [rows[m] * inverse[m] for m in range(PANEL)]
        for i in range(g + 1, len(tiles)):
            columns = []
            total = jnp.where(inside, 0.0, tiles[i])
            for m in range(PANEL):
                column = over_lanes(tiles[i], first + m)
                for l in range(m):
                    column = column - ratio[l][m] * columns[l]
                columns.append(column)
                total = total - column * scaled[m]
            tiles[i] = total
        squared, own = inverse[0], rows[0]
        for m in range(1, PANEL):
            squared = jnp.where(sub == m, inverse[m], squared)
            own = jnp.where(sub == m, rows[m], own)
        tiles[g] = own * (squared * lax.rsqrt(squared))
    return tiles


def inverse_factor_kernel(core_ref, mine_ref, other_ref, out_ref, work):
    n = out_ref.shape[0]
    half = n // 2
    for core, ref in ((core_ref[0], mine_ref), (1 - core_ref[0], other_ref)):
        work[pl.ds(pl.multiple_of(core * half, half), half), :] = ref[...]
    row_at = lax.broadcasted_iota(jnp.int32, (n, n), 0)
    col_at = lax.broadcasted_iota(jnp.int32, (n, n), 1)
    gram = work[...]
    diagonal = jnp.where(row_at == col_at, gram, 0.0)
    scale_cols = lax.rsqrt(jnp.sum(diagonal, axis=0, keepdims=True))
    scale_rows = lax.rsqrt(jnp.sum(diagonal, axis=1, keepdims=True))
    work[...] = gram * (scale_rows * scale_cols)

    def step(k, carry):
        first = pl.multiple_of(k * BLOCK, BLOCK)
        own = pl.ds(first, BLOCK)
        block = work[own, own]
        tiles = factor_block([block[PANEL * i : PANEL * (i + 1), :] for i in range(BLOCK // PANEL)])
        ri = lax.broadcasted_iota(jnp.int32, (BLOCK, BLOCK), 0)
        ci = lax.broadcasted_iota(jnp.int32, (BLOCK, BLOCK), 1)
        lower_inverse = jnp.where(ci <= ri, jnp.concatenate(tiles, axis=0), 0.0)
        work[own, own] = jnp.where(ci == ri, 1.0, 0.0)
        work[own, :] = jnp.dot(lower_inverse, work[own, :], precision=HIGHEST, preferred_element_type=F32)
        for at in range(BLOCK, n, BLOCK):

            @pl.when(first + BLOCK == at)
            def _():
                done = slice(at - BLOCK, at)
                work[at:, done] = jnp.zeros((n - at, BLOCK), F32)
                work[at:, :] -= lax.dot_general(
                    work[done, at:],
                    work[done, :],
                    (((0,), (0,)), ((), ())),
                    precision=HIGHEST,
                    preferred_element_type=F32,
                )

        return carry

    lax.fori_loop(0, n // BLOCK, step, 0)
    out_ref[...] = jnp.where(col_at <= row_at, work[...], 0.0) * scale_cols


def inverse_factor(core, mine, other):
    n = mine.shape[1]
    vmem = pl.BlockSpec(memory_space=pltpu.VMEM)
    return pl.pallas_call(
        inverse_factor_kernel,
        in_specs=[pl.BlockSpec(memory_space=pltpu.SMEM), vmem, vmem],
        out_specs=vmem,
        out_shape=jax.ShapeDtypeStruct((n, n), F32),
        scratch_shapes=[pltpu.VMEM((n, n), F32)],
        compiler_params=pltpu.CompilerParams(vmem_limit_bytes=16 << 20),
        cost_estimate=pl.CostEstimate(flops=2 * n**3, bytes_accessed=8 * n * n, transcendentals=4 * n),
    )(jnp.full((1,), core, jnp.int32), mine, other)


def this_core():
    return lax.rem(lax.axis_index("row"), 2)


def pick(array, at):
    return lax.dynamic_index_in_dim(array, lax.rem(at, array.shape[0]), 0, keepdims=False)


def swap_cores(array):
    return lax.ppermute(array, "row", [(i, i ^ 1) for i in range(lax.axis_size("row"))])


def send_col(array, step):
    size = lax.axis_size("col")
    return lax.ppermute(array, "col", [(i, (i + step) % size) for i in range(size)])


def flip_col(array, bits):
    return lax.ppermute(array, "col", [(i, i ^ bits) for i in range(lax.axis_size("col"))])


def exchange(pieces):
    rows = lax.axis_size("row")
    groups = [list(range(core, rows, 2)) for core in range(2)]
    return lax.all_to_all(pieces, "row", 0, 0, tiled=True, axis_index_groups=groups)


def spread(share):
    chips = lax.axis_size("row") // 2
    return exchange(lax.optimization_barrier(jnp.broadcast_to(share[None], (chips,) + share.shape)))


def sum_gram(share):
    core, chips = this_core(), lax.axis_size("row") // 2
    part = lax.dot_general(
        share, share, (((0,), (0,)), ((), ())), precision=HIGHEST, preferred_element_type=F32
    )
    n = part.shape[0]
    part = part.reshape(2, n // 2, n)
    half = pick(part, core) + swap_cores(pick(part, 1 - core))
    own = jnp.sum(exchange(half.reshape(chips, n // (2 * chips), n)), axis=0)
    total = own + flip_col(own, 1)
    total = (total + flip_col(total, 2)) + (flip_col(total, 4) + flip_col(total, 6))
    mine = spread(total).reshape(n // 2, n)
    return total, mine, swap_cores(mine)


def sum_cols(partial):
    size = lax.axis_size("col")
    me = lax.axis_index("col")
    blocks = partial.reshape(size, 2, partial.shape[0] // (2 * size), partial.shape[1])
    far = size // 2
    halves = []
    for half in range(2):
        own = pick(blocks[:, half], me)
        for way in (1, -1):
            hops = far if (way == 1) == (half == 0) else size - 1 - far
            moving = pick(blocks[:, half], me + size + way * hops)
            for left in range(hops - 1, -1, -1):
                moving = send_col(moving, way)
                if left > 0:
                    moving = moving + pick(blocks[:, half], me + size + way * left)
            own = own + moving
        halves.append(own)
    return jnp.concatenate(halves, axis=0)


def sum_rows(partial):
    core = this_core()
    pair = pick(partial, core) + swap_cores(pick(partial, 1 - core).astype(BF16)).astype(F32)
    return jnp.sum(exchange(pair.astype(BF16)).astype(F32), axis=0)


def gather_rows(share):
    core = this_core()
    mine = spread(share)
    other = swap_cores(mine)
    return jnp.where(core == 0, jnp.stack([mine, other]), jnp.stack([other, mine]))


def factor(partial):
    share = sum_cols(partial)
    total, mine, other = sum_gram(share)
    share, total = lax.optimization_barrier((share, total))
    sampled = lax.all_gather(share, "col", axis=0, tiled=True)
    return sampled, inverse_factor(this_core(), mine, other)


def times_transposed(sampled, lower_inverse):
    return lax.dot_general(
        sampled, lower_inverse, (((1,), (1,)), ((), ())), precision=HIGHEST, preferred_element_type=F32
    )


def body(activations, sketch):
    rows_dev, cols_dev = activations.shape
    rank = sketch.shape[1]
    row_count = lax.axis_size("row")
    chips = row_count // 2
    share = rank // row_count
    contract_rows = (((0,), (0,)), ((), ()))
    sampled, lower_inverse = factor(jnp.dot(activations, sketch, preferred_element_type=F32))
    basis_half = times_transposed(sampled, lower_inverse).astype(BF16)
    partial_sum = lax.dot_general(basis_half, activations, contract_rows, preferred_element_type=F32)
    own = sum_rows(partial_sum.reshape(2, chips, share, cols_dev)).astype(BF16)
    gathered = gather_rows(own).reshape(rank, cols_dev)
    sampled, lower_inverse = factor(
        lax.dot_general(activations, gathered, (((1,), (1,)), ((), ())), preferred_element_type=F32)
    )
    basis_half = times_transposed(sampled, lower_inverse).astype(BF16)
    projected = lax.dot_general(basis_half, activations, contract_rows, preferred_element_type=F32)
    projected = projected.reshape(chips, 2, share, cols_dev).swapaxes(0, 1)
    coefficients = sum_rows(projected)
    sampled, lower_inverse = lax.optimization_barrier((sampled, lower_inverse))
    scaled_basis = math.sqrt(rows_dev * row_count) * times_transposed(sampled, lower_inverse)
    return (scaled_basis, coefficients)


def solution(mesh):
    in_specs = (P("row", "col"), P("col", None))
    out_specs = (P("row", None), P("row", "col"))
    return jax.shard_map(body, mesh=mesh, in_specs=in_specs, out_specs=out_specs, check_vma=False)
```

```python
import functools
import math

import jax
import jax.numpy as jnp
from jax import lax
from jax.experimental import pallas as pl
from jax.experimental.pallas import tpu as pltpu
from jax.sharding import PartitionSpec as P

F32 = jnp.float32
BF16 = jnp.bfloat16
HIGHEST = lax.Precision.HIGHEST
BLOCK = 128
PANEL = 8


def factor_block(tiles):
    lane = lax.broadcasted_iota(jnp.int32, (PANEL, BLOCK), 1)
    sub = lax.broadcasted_iota(jnp.int32, (PANEL, BLOCK), 0)
    tiles = list(tiles)

    def over_lanes(tile, at):
        return jnp.broadcast_to(tile[:, at : at + 1], (PANEL, BLOCK))

    def over_rows(tile, at):
        return jnp.broadcast_to(tile[at : at + 1, :], (PANEL, BLOCK))

    for g in range(len(tiles)):
        first = PANEL * g
        pivot = [over_lanes(tiles[g], first + l) for l in range(PANEL)]
        entry = [[over_rows(pivot[l], m) for l in range(m + 1)] for m in range(PANEL)]
        ratio = [[None] * PANEL for _ in range(PANEL)]
        inverse = [None] * PANEL
        for j in range(PANEL):
            if j % 2 == 0:
                a, b, c = entry[j][j], entry[j + 1][j], entry[j + 1][j + 1]
                inverse[j] = 1.0 / a
                inverse[j + 1] = a * (1.0 / (a * c - b * b))
            for m in range(j + 1, PANEL):
                ratio[j][m] = entry[m][j] * inverse[j]
            for m in range(j + 1, PANEL):
                for l in range(j + 1, m + 1):
                    entry[m][l] = entry[m][l] - entry[m][j] * ratio[j][l]
        inside = (lane >= first) & (lane < first + PANEL)
        start = jnp.where(inside, jnp.where(lane == sub + first, 1.0, 0.0), tiles[g])
        rows = []
        for m in range(PANEL):
            row = over_rows(start, m)
            for l in range(m):
                row = row - ratio[l][m] * rows[l]
            rows.append(row)
        scaled = [rows[m] * inverse[m] for m in range(PANEL)]
        for i in range(g + 1, len(tiles)):
            columns = []
            total = jnp.where(inside, 0.0, tiles[i])
            for m in range(PANEL):
                column = over_lanes(tiles[i], first + m)
                for l in range(m):
                    column = column - ratio[l][m] * columns[l]
                columns.append(column)
                total = total - column * scaled[m]
            tiles[i] = total
        squared, own = inverse[0], rows[0]
        for m in range(1, PANEL):
            squared = jnp.where(sub == m, inverse[m], squared)
            own = jnp.where(sub == m, rows[m], own)
        tiles[g] = own * (squared * lax.rsqrt(squared))
    return tiles


def inverse_factor_kernel(chunk, core_ref, mine_ref, other_ref, out_ref, turned_ref, work):
    n = out_ref.shape[0]
    half = n // 2
    own, far = (pl.ds(pl.multiple_of(core * half, half), half) for core in (core_ref[0], 1 - core_ref[0]))
    work[own, own] = mine_ref[:, :half]
    work[own, far] = mine_ref[:, half:]
    work[far, far] = other_ref[:, :half]
    work[far, own] = other_ref[:, half:]
    row_at = lax.broadcasted_iota(jnp.int32, (n, n), 0)
    col_at = lax.broadcasted_iota(jnp.int32, (n, n), 1)
    gram = work[...]
    diagonal = jnp.where(row_at == col_at, gram, 0.0)
    scale_cols = lax.rsqrt(jnp.sum(diagonal, axis=0, keepdims=True))
    scale_rows = lax.rsqrt(jnp.sum(diagonal, axis=1, keepdims=True))
    work[...] = gram * (scale_rows * scale_cols)

    def step(k, carry):
        first = pl.multiple_of(k * BLOCK, BLOCK)
        here = pl.ds(first, BLOCK)
        block = work[here, here]
        tiles = factor_block([block[PANEL * i : PANEL * (i + 1), :] for i in range(BLOCK // PANEL)])
        ri = lax.broadcasted_iota(jnp.int32, (BLOCK, BLOCK), 0)
        ci = lax.broadcasted_iota(jnp.int32, (BLOCK, BLOCK), 1)
        lower_inverse = jnp.where(ci <= ri, jnp.concatenate(tiles, axis=0), 0.0)
        work[here, here] = jnp.where(ci == ri, 1.0, 0.0)
        work[here, :] = jnp.dot(lower_inverse, work[here, :], precision=HIGHEST, preferred_element_type=F32)
        for at in range(BLOCK, n, BLOCK):

            @pl.when(first + BLOCK == at)
            def _():
                done = slice(at - BLOCK, at)
                work[at:, done] = jnp.zeros((n - at, BLOCK), F32)
                work[at:, :] -= lax.dot_general(
                    work[done, at:],
                    work[done, :],
                    (((0,), (0,)), ((), ())),
                    precision=HIGHEST,
                    preferred_element_type=F32,
                )

        return carry

    lax.fori_loop(0, n // BLOCK, step, 0)
    work[...] = jnp.where(col_at <= row_at, work[...], 0.0) * scale_cols
    out_ref[:, :half] = work[:, own]
    out_ref[:, half:] = work[:, far]
    for i in range(half // chunk):
        for core, to in ((1 - core_ref[0], i * chunk), (core_ref[0], half + i * chunk)):
            rows = pl.ds(pl.multiple_of((2 * i + core) * chunk, chunk), chunk)
            turned_ref[to : to + chunk, :] = out_ref[rows, :]


def inverse_factor(core, mine, other, chunk):
    n = mine.shape[1]
    vmem = pl.BlockSpec(memory_space=pltpu.VMEM)
    return pl.pallas_call(
        functools.partial(inverse_factor_kernel, chunk),
        in_specs=[pl.BlockSpec(memory_space=pltpu.SMEM), vmem, vmem],
        out_specs=[vmem] * 2,
        out_shape=[jax.ShapeDtypeStruct((n, n), F32)] * 2,
        scratch_shapes=[pltpu.VMEM((n, n), F32)],
        compiler_params=pltpu.CompilerParams(vmem_limit_bytes=16 << 20),
        cost_estimate=pl.CostEstimate(flops=2 * n**3, bytes_accessed=8 * n * n, transcendentals=4 * n),
    )(jnp.full((1,), core, jnp.int32), mine, other)


def product_kernel(transposed, at_ref, left_ref, right_ref, out_ref):
    cols = out_ref.shape[1]
    right = right_ref[...] if transposed else right_ref[:, pl.ds(pl.multiple_of(at_ref[0] * cols, cols), cols)]
    out_ref[...] = lax.dot_general(
        left_ref[...], right, (((1,), (int(transposed),)), ((), ())), preferred_element_type=F32
    )


def product(left, right, cols, at=0, transposed=False):
    rows, depth = left.shape
    tile = min(rows, 256)
    return pl.pallas_call(
        functools.partial(product_kernel, transposed),
        grid=(rows // tile,),
        in_specs=[
            pl.BlockSpec(memory_space=pltpu.SMEM),
            pl.BlockSpec((tile, depth), lambda i: (i, 0)),
            pl.BlockSpec(right.shape, lambda i: (0, 0)),
        ],
        out_specs=pl.BlockSpec((tile, cols), lambda i: (i, 0)),
        out_shape=jax.ShapeDtypeStruct((rows, cols), F32),
        compiler_params=pltpu.CompilerParams(vmem_limit_bytes=16 << 20),
        cost_estimate=pl.CostEstimate(
            flops=2 * rows * cols * depth,
            bytes_accessed=2 * (rows + cols) * depth + 4 * rows * cols,
            transcendentals=0,
        ),
    )(jnp.full((1,), at, jnp.int32), left, right)


def this_core():
    return lax.rem(lax.axis_index("row"), 2)


def pick(array, at):
    return lax.dynamic_index_in_dim(array, lax.rem(at, array.shape[0]), 0, keepdims=False)


def swap_cores(array):
    return lax.ppermute(array, "row", [(i, i ^ 1) for i in range(lax.axis_size("row"))])


def send_col(array, step):
    size = lax.axis_size("col")
    return lax.ppermute(array, "col", [(i, (i + step) % size) for i in range(size)])


def flip_col(array, bits):
    return lax.ppermute(array, "col", [(i, i ^ bits) for i in range(lax.axis_size("col"))])


def exchange(pieces):
    rows = lax.axis_size("row")
    groups = [list(range(core, rows, 2)) for core in range(2)]
    return lax.all_to_all(pieces, "row", 0, 0, tiled=True, axis_index_groups=groups)


def spread(share):
    chips = lax.axis_size("row") // 2
    return exchange(lax.optimization_barrier(jnp.broadcast_to(share[None], (chips,) + share.shape)))


def sum_gram(share):
    chips = lax.axis_size("row") // 2
    n = share.shape[1]
    other = swap_cores(share)
    both = jnp.concatenate([share, jnp.concatenate([other[:, n // 2 :], other[:, : n // 2]], axis=1)])
    half = lax.dot_general(
        both[:, : n // 2], both, (((0,), (0,)), ((), ())), precision=HIGHEST, preferred_element_type=F32
    )
    own = jnp.sum(exchange(half.reshape(chips, n // (2 * chips), n)), axis=0)
    pair = own + flip_col(own, 1)
    total = (pair + flip_col(pair, 2)) + (flip_col(pair, 4) + flip_col(pair, 6))
    mine = spread(total).reshape(n // 2, n)
    return pair, mine, swap_cores(mine)


def sum_cols(partials):
    size = lax.axis_size("col")
    me = lax.axis_index("col")
    far = size // 2
    sums = []
    for at, partial in enumerate(partials):
        blocks = partial.reshape(size, partial.shape[0] // size, partial.shape[1])
        own = pick(blocks, me)
        for way in (1, -1):
            hops = far if (way == 1) == (at == 0) else size - 1 - far
            moving = pick(blocks, me + size + way * hops)
            for left in range(hops - 1, -1, -1):
                moving = send_col(moving, way)
                if left > 0:
                    moving = moving + pick(blocks, me + size + way * left)
            own = own + moving
        sums.append(own)
    return jnp.concatenate(sums, axis=1)


def factor(partials, chunk):
    share = sum_cols(partials)
    pair, mine, other = sum_gram(share)
    share, _ = lax.optimization_barrier((share, pair))
    sampled = lax.all_gather(share, "col", axis=0, tiled=True)
    return sampled, inverse_factor(this_core(), mine, other, chunk)


def times_transposed(sampled, lower_inverse):
    return lax.dot_general(
        sampled, lower_inverse, (((1,), (1,)), ((), ())), precision=HIGHEST, preferred_element_type=F32
    )


def project(sampled, turned, activations):
    chips = lax.axis_size("row") // 2
    basis_half = times_transposed(sampled, turned).astype(BF16)
    n = basis_half.shape[1] // 2

    def half(columns):
        return lax.dot_general(
            columns, activations, (((0,), (0,)), ((), ())), preferred_element_type=F32
        )

    arrived = swap_cores(half(basis_half[:, :n]).astype(BF16))
    stay = lax.optimization_barrier(half(basis_half[:, n:]))
    pair = (stay + arrived.astype(F32)).astype(BF16)
    return jnp.sum(exchange(pair.reshape(chips, n // chips, pair.shape[1])).astype(F32), axis=0)


def body(activations, sketch):
    rows_dev, cols_dev = activations.shape
    rank = sketch.shape[1]
    row_count = lax.axis_size("row")
    half = rank // 2
    core = this_core()
    partials = [product(activations, sketch, half, at) for at in (core, 1 - core)]
    sampled, (_, turned) = factor(partials, half)
    share = project(sampled, turned, activations).astype(BF16)
    mine = spread(share).reshape(half, cols_dev)
    partials = [product(activations, gathered, half, transposed=True) for gathered in (mine, swap_cores(mine))]
    sampled, (lower_inverse, turned) = factor(partials, rank // row_count)
    coefficients = project(sampled, turned, activations)
    sampled, lower_inverse = lax.optimization_barrier((sampled, lower_inverse))
    scaled_basis = math.sqrt(rows_dev * row_count) * times_transposed(sampled, lower_inverse)
    return (scaled_basis, coefficients)


def solution(mesh):
    in_specs = (P("row", "col"), P("col", None))
    out_specs = (P("row", None), P("row", "col"))
    return jax.shard_map(body, mesh=mesh, in_specs=in_specs, out_specs=out_specs, check_vma=False)
```

```python
import functools
import math

import jax
import jax.numpy as jnp
from jax import lax
from jax.experimental import pallas as pl
from jax.experimental.pallas import tpu as pltpu
from jax.sharding import PartitionSpec as P

F32 = jnp.float32
BF16 = jnp.bfloat16
HIGHEST = lax.Precision.HIGHEST
BLOCK = 128
PANEL = 8


def factor_block(tiles):
    lane = lax.broadcasted_iota(jnp.int32, (PANEL, BLOCK), 1)
    sub = lax.broadcasted_iota(jnp.int32, (PANEL, BLOCK), 0)
    tiles = list(tiles)

    def over_lanes(tile, at):
        return jnp.broadcast_to(tile[:, at : at + 1], (PANEL, BLOCK))

    def over_rows(tile, at):
        return jnp.broadcast_to(tile[at : at + 1, :], (PANEL, BLOCK))

    for g in range(len(tiles)):
        first = PANEL * g
        pivot = [over_lanes(tiles[g], first + l) for l in range(PANEL)]
        entry = [[over_rows(pivot[l], m) for l in range(m + 1)] for m in range(PANEL)]
        ratio = [[None] * PANEL for _ in range(PANEL)]
        inverse = [None] * PANEL
        for j in range(PANEL):
            if j % 2 == 0:
                a, b, c = entry[j][j], entry[j + 1][j], entry[j + 1][j + 1]
                inverse[j] = 1.0 / a
                inverse[j + 1] = a * (1.0 / (a * c - b * b))
            for m in range(j + 1, PANEL):
                ratio[j][m] = entry[m][j] * inverse[j]
            for m in range(j + 1, PANEL):
                for l in range(j + 1, m + 1):
                    entry[m][l] = entry[m][l] - entry[m][j] * ratio[j][l]
        inside = (lane >= first) & (lane < first + PANEL)
        start = jnp.where(inside, jnp.where(lane == sub + first, 1.0, 0.0), tiles[g])
        rows = []
        for m in range(PANEL):
            row = over_rows(start, m)
            for l in range(m):
                row = row - ratio[l][m] * rows[l]
            rows.append(row)
        scaled = [rows[m] * inverse[m] for m in range(PANEL)]
        for i in range(g + 1, len(tiles)):
            columns = []
            total = jnp.where(inside, 0.0, tiles[i])
            for m in range(PANEL):
                column = over_lanes(tiles[i], first + m)
                for l in range(m):
                    column = column - ratio[l][m] * columns[l]
                columns.append(column)
                total = total - column * scaled[m]
            tiles[i] = total
        squared, own = inverse[0], rows[0]
        for m in range(1, PANEL):
            squared = jnp.where(sub == m, inverse[m], squared)
            own = jnp.where(sub == m, rows[m], own)
        tiles[g] = own * (squared * lax.rsqrt(squared))
    return tiles


def inverse_factor_kernel(chunk, core_ref, mine_ref, other_ref, turned_ref, *rest):
    *out_ref, work = rest
    n = work.shape[0]
    half = n // 2
    own, far = (pl.ds(pl.multiple_of(core * half, half), half) for core in (core_ref[0], 1 - core_ref[0]))
    work[own, own] = mine_ref[:, :half]
    work[own, far] = mine_ref[:, half:]
    work[far, far] = other_ref[:, :half]
    work[far, own] = other_ref[:, half:]
    row_at = lax.broadcasted_iota(jnp.int32, (n, n), 0)
    col_at = lax.broadcasted_iota(jnp.int32, (n, n), 1)
    gram = work[...]
    diagonal = jnp.where(row_at == col_at, gram, 0.0)
    scale_cols = lax.rsqrt(jnp.sum(diagonal, axis=0, keepdims=True))
    scale_rows = lax.rsqrt(jnp.sum(diagonal, axis=1, keepdims=True))
    work[...] = gram * (scale_rows * scale_cols)

    def step(k, carry):
        first = pl.multiple_of(k * BLOCK, BLOCK)
        here = pl.ds(first, BLOCK)
        block = work[here, here]
        tiles = factor_block([block[PANEL * i : PANEL * (i + 1), :] for i in range(BLOCK // PANEL)])
        ri = lax.broadcasted_iota(jnp.int32, (BLOCK, BLOCK), 0)
        ci = lax.broadcasted_iota(jnp.int32, (BLOCK, BLOCK), 1)
        lower_inverse = jnp.where(ci <= ri, jnp.concatenate(tiles, axis=0), 0.0)
        work[here, here] = jnp.where(ci == ri, 1.0, 0.0)
        work[here, :] = jnp.dot(lower_inverse, work[here, :], precision=HIGHEST, preferred_element_type=F32)
        for at in range(BLOCK, n, BLOCK):

            @pl.when(first + BLOCK == at)
            def _():
                done = slice(at - BLOCK, at)
                work[at:, done] = jnp.zeros((n - at, BLOCK), F32)
                work[at:, :] -= lax.dot_general(
                    work[done, at:],
                    work[done, :],
                    (((0,), (0,)), ((), ())),
                    precision=HIGHEST,
                    preferred_element_type=F32,
                )

        return carry

    lax.fori_loop(0, n // BLOCK, step, 0)
    work[...] = jnp.where(col_at <= row_at, work[...], 0.0) * scale_cols
    for ref in out_ref:
        ref[:, :half] = work[:, own]
        ref[:, half:] = work[:, far]
    for i in range(half // chunk):
        for core, to in ((1 - core_ref[0], i * chunk), (core_ref[0], half + i * chunk)):
            rows = pl.ds(pl.multiple_of((2 * i + core) * chunk, chunk), chunk)
            turned_ref[to : to + chunk, :half] = work[rows, own]
            turned_ref[to : to + chunk, half:] = work[rows, far]


def inverse_factor(core, mine, other, chunk, whole):
    n = mine.shape[1]
    vmem = pl.BlockSpec(memory_space=pltpu.VMEM)
    return pl.pallas_call(
        functools.partial(inverse_factor_kernel, chunk),
        in_specs=[pl.BlockSpec(memory_space=pltpu.SMEM), vmem, vmem],
        out_specs=[vmem] * (1 + whole),
        out_shape=[jax.ShapeDtypeStruct((n, n), F32)] * (1 + whole),
        scratch_shapes=[pltpu.VMEM((n, n), F32)],
        compiler_params=pltpu.CompilerParams(vmem_limit_bytes=16 << 20),
        cost_estimate=pl.CostEstimate(flops=2 * n**3, bytes_accessed=8 * n * n, transcendentals=4 * n),
    )(jnp.full((1,), core, jnp.int32), mine, other)


def product_kernel(transposed, at_ref, left_ref, right_ref, out_ref):
    cols = out_ref.shape[1]
    right = right_ref[...] if transposed else right_ref[:, pl.ds(pl.multiple_of(at_ref[0] * cols, cols), cols)]
    out_ref[...] = lax.dot_general(
        left_ref[...], right, (((1,), (int(transposed),)), ((), ())), preferred_element_type=F32
    )


def product(left, right, cols, at=0, transposed=False):
    rows, depth = left.shape
    tile = min(rows, 256)
    return pl.pallas_call(
        functools.partial(product_kernel, transposed),
        grid=(rows // tile,),
        in_specs=[
            pl.BlockSpec(memory_space=pltpu.SMEM),
            pl.BlockSpec((tile, depth), lambda i: (i, 0)),
            pl.BlockSpec(right.shape, lambda i: (0, 0)),
        ],
        out_specs=pl.BlockSpec((tile, cols), lambda i: (i, 0)),
        out_shape=jax.ShapeDtypeStruct((rows, cols), F32),
        compiler_params=pltpu.CompilerParams(vmem_limit_bytes=16 << 20),
        cost_estimate=pl.CostEstimate(
            flops=2 * rows * cols * depth,
            bytes_accessed=2 * (rows + cols) * depth + 4 * rows * cols,
            transcendentals=0,
        ),
    )(jnp.full((1,), at, jnp.int32), left, right)


def this_core():
    return lax.rem(lax.axis_index("row"), 2)


def pick(array, at):
    return lax.dynamic_index_in_dim(array, lax.rem(at, array.shape[0]), 0, keepdims=False)


def swap_cores(array):
    return lax.ppermute(array, "row", [(i, i ^ 1) for i in range(lax.axis_size("row"))])


def send_col(array, step):
    size = lax.axis_size("col")
    return lax.ppermute(array, "col", [(i, (i + step) % size) for i in range(size)])


def flip_col(array, bits):
    return lax.ppermute(array, "col", [(i, i ^ bits) for i in range(lax.axis_size("col"))])


def exchange(pieces):
    rows = lax.axis_size("row")
    groups = [list(range(core, rows, 2)) for core in range(2)]
    return lax.all_to_all(pieces, "row", 0, 0, tiled=True, axis_index_groups=groups)


def spread(share):
    chips = lax.axis_size("row") // 2
    return exchange(lax.optimization_barrier(jnp.broadcast_to(share[None], (chips,) + share.shape)))


def sum_gram(share):
    chips = lax.axis_size("row") // 2
    n = share.shape[1]
    other = swap_cores(share)
    both = jnp.concatenate([share, jnp.concatenate([other[:, n // 2 :], other[:, : n // 2]], axis=1)])
    half = lax.dot_general(
        both[:, : n // 2], both, (((0,), (0,)), ((), ())), precision=HIGHEST, preferred_element_type=F32
    )
    own = jnp.sum(exchange(half.reshape(chips, n // (2 * chips), n)), axis=0)
    pair = own + flip_col(own, 1)
    total = (pair + flip_col(pair, 2)) + (flip_col(pair, 4) + flip_col(pair, 6))
    mine = spread(total).reshape(n // 2, n)
    return pair, mine, swap_cores(mine)


def sum_cols(partials):
    size = lax.axis_size("col")
    me = lax.axis_index("col")
    far = size // 2
    sums = []
    for at, partial in enumerate(partials):
        blocks = partial.reshape(size, partial.shape[0] // size, partial.shape[1])
        own = pick(blocks, me)
        for way in (1, -1):
            hops = far if (way == 1) == (at == 0) else size - 1 - far
            moving = pick(blocks, me + size + way * hops)
            for left in range(hops - 1, -1, -1):
                moving = send_col(moving, way)
                if left > 0:
                    moving = moving + pick(blocks, me + size + way * left)
            own = own + moving
        sums.append(own)
    return jnp.concatenate(sums, axis=1)


def factor(partials, chunk, whole):
    share = sum_cols(partials)
    pair, mine, other = sum_gram(share)
    share, _ = lax.optimization_barrier((share, pair))
    sampled = lax.all_gather(share, "col", axis=0, tiled=True)
    return sampled, inverse_factor(this_core(), mine, other, chunk, whole)


def times_transposed(sampled, lower_inverse, precision):
    return lax.dot_general(
        sampled, lower_inverse, (((1,), (1,)), ((), ())), precision=precision, preferred_element_type=F32
    )


def project(sampled, turned, activations, precision):
    chips = lax.axis_size("row") // 2
    basis_half = times_transposed(sampled, turned, precision).astype(BF16)
    n = basis_half.shape[1] // 2

    def half(columns):
        return lax.dot_general(
            columns, activations, (((0,), (0,)), ((), ())), preferred_element_type=F32
        )

    arrived = swap_cores(half(basis_half[:, :n]).astype(BF16))
    stay = lax.optimization_barrier(half(basis_half[:, n:]))
    pair = (stay + arrived.astype(F32)).astype(BF16)
    return jnp.sum(exchange(pair.reshape(chips, n // chips, pair.shape[1])).astype(F32), axis=0)


def body(activations, sketch):
    rows_dev, cols_dev = activations.shape
    rank = sketch.shape[1]
    row_count = lax.axis_size("row")
    half = rank // 2
    core = this_core()
    partials = [product(activations, sketch, half, at) for at in (core, 1 - core)]
    sampled, (turned,) = factor(partials, half, False)
    share = project(sampled, turned, activations, HIGHEST).astype(BF16)
    mine = spread(share).reshape(half, cols_dev)
    partials = [product(activations, gathered, half, transposed=True) for gathered in (mine, swap_cores(mine))]
    sampled, (turned, lower_inverse) = factor(partials, rank // row_count, True)
    coefficients = project(sampled, turned, activations, lax.Precision.HIGH)
    sampled, lower_inverse = lax.optimization_barrier((sampled, lower_inverse))
    scaled_basis = math.sqrt(rows_dev * row_count) * times_transposed(sampled, lower_inverse, HIGHEST)
    return (scaled_basis, coefficients)


def solution(mesh):
    in_specs = (P("row", "col"), P("col", None))
    out_specs = (P("row", None), P("row", "col"))
    return jax.shard_map(body, mesh=mesh, in_specs=in_specs, out_specs=out_specs, check_vma=False)
```

```python
import functools
import math

import jax
import jax.numpy as jnp
from jax import lax
from jax.experimental import pallas as pl
from jax.experimental.pallas import tpu as pltpu
from jax.sharding import PartitionSpec as P

F32 = jnp.float32
BF16 = jnp.bfloat16
HIGHEST = lax.Precision.HIGHEST
HIGH = lax.Precision.HIGH
BLOCK = 128
PANEL = 8


def factor_block(tiles):
    lane = lax.broadcasted_iota(jnp.int32, (PANEL, BLOCK), 1)
    sub = lax.broadcasted_iota(jnp.int32, (PANEL, BLOCK), 0)
    tiles = list(tiles)

    def over_lanes(tile, at):
        return jnp.broadcast_to(tile[:, at : at + 1], (PANEL, BLOCK))

    def over_rows(tile, at):
        return jnp.broadcast_to(tile[at : at + 1, :], (PANEL, BLOCK))

    for g in range(len(tiles)):
        first = PANEL * g
        pivot = [over_lanes(tiles[g], first + l) for l in range(PANEL)]
        entry = [[over_rows(pivot[l], m) for l in range(m + 1)] for m in range(PANEL)]
        ratio = [[None] * PANEL for _ in range(PANEL)]
        inverse = [None] * PANEL
        for j in range(PANEL):
            if j % 2 == 0:
                a, b, c = entry[j][j], entry[j + 1][j], entry[j + 1][j + 1]
                inverse[j] = 1.0 / a
                inverse[j + 1] = a * (1.0 / (a * c - b * b))
            for m in range(j + 1, PANEL):
                ratio[j][m] = entry[m][j] * inverse[j]
            for m in range(j + 1, PANEL):
                for l in range(j + 1, m + 1):
                    entry[m][l] = entry[m][l] - entry[m][j] * ratio[j][l]
        inside = (lane >= first) & (lane < first + PANEL)
        start = jnp.where(inside, jnp.where(lane == sub + first, 1.0, 0.0), tiles[g])
        rows = []
        for m in range(PANEL):
            row = over_rows(start, m)
            for l in range(m):
                row = row - ratio[l][m] * rows[l]
            rows.append(row)
        scaled = [rows[m] * inverse[m] for m in range(PANEL)]
        for i in range(g + 1, len(tiles)):
            columns = []
            total = jnp.where(inside, 0.0, tiles[i])
            for m in range(PANEL):
                column = over_lanes(tiles[i], first + m)
                for l in range(m):
                    column = column - ratio[l][m] * columns[l]
                columns.append(column)
                total = total - column * scaled[m]
            tiles[i] = total
        squared, own = inverse[0], rows[0]
        for m in range(1, PANEL):
            squared = jnp.where(sub == m, inverse[m], squared)
            own = jnp.where(sub == m, rows[m], own)
        tiles[g] = own * (squared * lax.rsqrt(squared))
    return tiles


def inverse_factor_kernel(chunk, core_ref, mine_ref, other_ref, turned_ref, *rest):
    *out_ref, work = rest
    n = work.shape[0]
    half = n // 2
    own, far = (pl.ds(pl.multiple_of(core * half, half), half) for core in (core_ref[0], 1 - core_ref[0]))
    work[own, own] = mine_ref[:, :half]
    work[own, far] = mine_ref[:, half:]
    work[far, far] = other_ref[:, :half]
    work[far, own] = other_ref[:, half:]
    row_at = lax.broadcasted_iota(jnp.int32, (n, n), 0)
    col_at = lax.broadcasted_iota(jnp.int32, (n, n), 1)
    gram = work[...]
    diagonal = jnp.where(row_at == col_at, gram, 0.0)
    scale_cols = lax.rsqrt(jnp.sum(diagonal, axis=0, keepdims=True))
    scale_rows = lax.rsqrt(jnp.sum(diagonal, axis=1, keepdims=True))
    work[...] = gram * (scale_rows * scale_cols)

    def step(k, carry):
        first = pl.multiple_of(k * BLOCK, BLOCK)
        here = pl.ds(first, BLOCK)
        block = work[here, here]
        tiles = factor_block([block[PANEL * i : PANEL * (i + 1), :] for i in range(BLOCK // PANEL)])
        ri = lax.broadcasted_iota(jnp.int32, (BLOCK, BLOCK), 0)
        ci = lax.broadcasted_iota(jnp.int32, (BLOCK, BLOCK), 1)
        lower_inverse = jnp.where(ci <= ri, jnp.concatenate(tiles, axis=0), 0.0)
        work[here, here] = jnp.where(ci == ri, 1.0, 0.0)
        work[here, :] = jnp.dot(lower_inverse, work[here, :], precision=HIGHEST, preferred_element_type=F32)
        for at in range(BLOCK, n, BLOCK):

            @pl.when(first + BLOCK == at)
            def _():
                done = slice(at - BLOCK, at)
                work[at:, done] = jnp.zeros((n - at, BLOCK), F32)
                work[at:, :] -= lax.dot_general(
                    work[done, at:],
                    work[done, :],
                    (((0,), (0,)), ((), ())),
                    precision=HIGHEST,
                    preferred_element_type=F32,
                )

        return carry

    lax.fori_loop(0, n // BLOCK, step, 0)
    work[...] = jnp.where(col_at <= row_at, work[...], 0.0) * scale_cols
    for ref in out_ref:
        ref[:, :half] = work[:, own]
        ref[:, half:] = work[:, far]
    for i in range(half // chunk):
        for core, to in ((1 - core_ref[0], i * chunk), (core_ref[0], half + i * chunk)):
            rows = pl.ds(pl.multiple_of((2 * i + core) * chunk, chunk), chunk)
            turned_ref[to : to + chunk, :half] = work[rows, own]
            turned_ref[to : to + chunk, half:] = work[rows, far]


def inverse_factor(core, mine, other, chunk, whole):
    n = mine.shape[1]
    vmem = pl.BlockSpec(memory_space=pltpu.VMEM)
    return pl.pallas_call(
        functools.partial(inverse_factor_kernel, chunk),
        in_specs=[pl.BlockSpec(memory_space=pltpu.SMEM), vmem, vmem],
        out_specs=[vmem] * (1 + whole),
        out_shape=[jax.ShapeDtypeStruct((n, n), F32)] * (1 + whole),
        scratch_shapes=[pltpu.VMEM((n, n), F32)],
        compiler_params=pltpu.CompilerParams(vmem_limit_bytes=16 << 20),
        cost_estimate=pl.CostEstimate(flops=2 * n**3, bytes_accessed=8 * n * n, transcendentals=4 * n),
    )(jnp.full((1,), core, jnp.int32), mine, other)


def product_kernel(transposed, at_ref, left_ref, right_ref, out_ref):
    cols = out_ref.shape[1]
    right = right_ref[...] if transposed else right_ref[:, pl.ds(pl.multiple_of(at_ref[0] * cols, cols), cols)]
    out_ref[...] = lax.dot_general(
        left_ref[...], right, (((1,), (int(transposed),)), ((), ())), preferred_element_type=F32
    )


def product(left, right, cols, at=0, transposed=False):
    rows, depth = left.shape
    tile = min(rows, 256)
    return pl.pallas_call(
        functools.partial(product_kernel, transposed),
        grid=(rows // tile,),
        in_specs=[
            pl.BlockSpec(memory_space=pltpu.SMEM),
            pl.BlockSpec((tile, depth), lambda i: (i, 0)),
            pl.BlockSpec(right.shape, lambda i: (0, 0)),
        ],
        out_specs=pl.BlockSpec((tile, cols), lambda i: (i, 0)),
        out_shape=jax.ShapeDtypeStruct((rows, cols), F32),
        compiler_params=pltpu.CompilerParams(vmem_limit_bytes=16 << 20),
        cost_estimate=pl.CostEstimate(
            flops=2 * rows * cols * depth,
            bytes_accessed=2 * (rows + cols) * depth + 4 * rows * cols,
            transcendentals=0,
        ),
    )(jnp.full((1,), at, jnp.int32), left, right)


def this_core():
    return lax.rem(lax.axis_index("row"), 2)


def pick(array, at):
    return lax.dynamic_index_in_dim(array, lax.rem(at, array.shape[0]), 0, keepdims=False)


def swap_cores(array):
    return lax.ppermute(array, "row", [(i, i ^ 1) for i in range(lax.axis_size("row"))])


def send_col(array, step):
    size = lax.axis_size("col")
    return lax.ppermute(array, "col", [(i, (i + step) % size) for i in range(size)])


def flip_col(array, bits):
    return lax.ppermute(array, "col", [(i, i ^ bits) for i in range(lax.axis_size("col"))])


def exchange(pieces):
    rows = lax.axis_size("row")
    groups = [list(range(core, rows, 2)) for core in range(2)]
    return lax.all_to_all(pieces, "row", 0, 0, tiled=True, axis_index_groups=groups)


def spread(share):
    chips = lax.axis_size("row") // 2
    return exchange(lax.optimization_barrier(jnp.broadcast_to(share[None], (chips,) + share.shape)))


def sum_gram(share):
    chips = lax.axis_size("row") // 2
    n = share.shape[1]
    other = swap_cores(share)
    both = jnp.concatenate([share, jnp.concatenate([other[:, n // 2 :], other[:, : n // 2]], axis=1)])
    half = lax.dot_general(
        both[:, : n // 2], both, (((0,), (0,)), ((), ())), precision=HIGHEST, preferred_element_type=F32
    )
    own = jnp.sum(exchange(half.reshape(chips, n // (2 * chips), n)), axis=0)
    pair = own + flip_col(own, 1)
    total = (pair + flip_col(pair, 2)) + (flip_col(pair, 4) + flip_col(pair, 6))
    mine = spread(total).reshape(n // 2, n)
    return pair, mine, swap_cores(mine)


def sum_cols(partials):
    size = lax.axis_size("col")
    me = lax.axis_index("col")
    far = size // 2
    sums = []
    for at, partial in enumerate(partials):
        blocks = partial.reshape(size, partial.shape[0] // size, partial.shape[1])
        own = pick(blocks, me)
        for way in (1, -1):
            hops = far if (way == 1) == (at == 0) else size - 1 - far
            moving = pick(blocks, me + size + way * hops)
            for left in range(hops - 1, -1, -1):
                moving = send_col(moving, way)
                if left > 0:
                    moving = moving + pick(blocks, me + size + way * left)
            own = own + moving
        sums.append(own)
    return jnp.concatenate(sums, axis=1)


def factor(partials, chunk, whole):
    share = sum_cols(partials)
    pair, mine, other = sum_gram(share)
    share, _ = lax.optimization_barrier((share, pair))
    sampled = lax.all_gather(share, "col", axis=0, tiled=True)
    return sampled, inverse_factor(this_core(), mine, other, chunk, whole)


def times_transposed(sampled, lower_inverse, precision):
    return lax.dot_general(
        sampled,
        lower_inverse,
        (((1,), (1,)), ((), ())),
        precision=precision,
        preferred_element_type=F32,
    )


def project(sampled, turned, activations, precision, beside):
    chips = lax.axis_size("row") // 2
    basis_half = times_transposed(sampled, turned, precision).astype(BF16)
    n = basis_half.shape[1] // 2

    def half(columns):
        return lax.dot_general(
            columns, activations, (((0,), (0,)), ((), ())), preferred_element_type=F32
        )

    arrived = swap_cores(half(basis_half[:, :n]).astype(BF16))
    stay, beside = lax.optimization_barrier((half(basis_half[:, n:]), beside))
    pair = (stay + arrived.astype(F32)).astype(BF16)
    pair, beside = lax.optimization_barrier((pair.reshape(chips, n // chips, pair.shape[1]), beside))
    return jnp.sum(exchange(pair).astype(F32), axis=0), beside


def body(activations, sketch):
    rows_dev, cols_dev = activations.shape
    rank = sketch.shape[1]
    row_count = lax.axis_size("row")
    half = rank // 2
    core = this_core()
    partials = [product(activations, sketch, half, at) for at in (core, 1 - core)]
    sampled, (turned,) = factor(partials, half, False)
    share, _ = project(sampled, turned, activations, HIGHEST, ())
    mine = spread(share.astype(BF16)).reshape(half, cols_dev)
    partials = [product(activations, gathered, half, transposed=True) for gathered in (mine, swap_cores(mine))]
    sampled, (turned, lower_inverse) = factor(partials, rank // row_count, True)
    scaled_basis = math.sqrt(rows_dev * row_count) * times_transposed(sampled, lower_inverse, HIGH)
    coefficients, scaled_basis = project(sampled, turned, activations, HIGH, scaled_basis)
    return (scaled_basis, coefficients)


def solution(mesh):
    in_specs = (P("row", "col"), P("col", None))
    out_specs = (P("row", None), P("row", "col"))
    return jax.shard_map(body, mesh=mesh, in_specs=in_specs, out_specs=out_specs, check_vma=False)
```

```python
import functools
import math

import jax
import jax.numpy as jnp
from jax import lax
from jax.experimental import pallas as pl
from jax.experimental.pallas import tpu as pltpu
from jax.sharding import PartitionSpec as P

F32 = jnp.float32
BF16 = jnp.bfloat16
HIGHEST = lax.Precision.HIGHEST
HIGH = lax.Precision.HIGH
BLOCK = 128
PANEL = 8


def factor_block(tiles):
    lane = lax.broadcasted_iota(jnp.int32, (PANEL, BLOCK), 1)
    sub = lax.broadcasted_iota(jnp.int32, (PANEL, BLOCK), 0)
    tiles = list(tiles)

    def over_lanes(tile, at):
        return jnp.broadcast_to(tile[:, at : at + 1], (PANEL, BLOCK))

    def over_rows(tile, at):
        return jnp.broadcast_to(tile[at : at + 1, :], (PANEL, BLOCK))

    for g in range(len(tiles)):
        first = PANEL * g
        pivot = [over_lanes(tiles[g], first + l) for l in range(PANEL)]
        entry = [[over_rows(pivot[l], m) for l in range(m + 1)] for m in range(PANEL)]
        ratio = [[None] * PANEL for _ in range(PANEL)]
        inverse = [None] * PANEL
        for j in range(PANEL):
            if j % 2 == 0:
                a, b, c = entry[j][j], entry[j + 1][j], entry[j + 1][j + 1]
                inverse[j] = 1.0 / a
                inverse[j + 1] = a * (1.0 / (a * c - b * b))
            for m in range(j + 1, PANEL):
                ratio[j][m] = entry[m][j] * inverse[j]
            for m in range(j + 1, PANEL):
                for l in range(j + 1, m + 1):
                    entry[m][l] = entry[m][l] - entry[m][j] * ratio[j][l]
        inside = (lane >= first) & (lane < first + PANEL)
        start = jnp.where(inside, jnp.where(lane == sub + first, 1.0, 0.0), tiles[g])
        rows = []
        for m in range(PANEL):
            row = over_rows(start, m)
            for l in range(m):
                row = row - ratio[l][m] * rows[l]
            rows.append(row)
        scaled = [rows[m] * inverse[m] for m in range(PANEL)]
        for i in range(g + 1, len(tiles)):
            columns = []
            total = jnp.where(inside, 0.0, tiles[i])
            for m in range(PANEL):
                column = over_lanes(tiles[i], first + m)
                for l in range(m):
                    column = column - ratio[l][m] * columns[l]
                columns.append(column)
                total = total - column * scaled[m]
            tiles[i] = total
        squared, own = inverse[0], rows[0]
        for m in range(1, PANEL):
            squared = jnp.where(sub == m, inverse[m], squared)
            own = jnp.where(sub == m, rows[m], own)
        tiles[g] = own * (squared * lax.rsqrt(squared))
    return tiles


def inverse_factor_kernel(chunk, core_ref, mine_ref, other_ref, turned_ref, *rest):
    *out_ref, work = rest
    n = work.shape[0]
    half = n // 2
    own, far = (pl.ds(pl.multiple_of(core * half, half), half) for core in (core_ref[0], 1 - core_ref[0]))
    work[own, own] = mine_ref[:, :half]
    work[own, far] = mine_ref[:, half:]
    work[far, far] = other_ref[:, :half]
    work[far, own] = other_ref[:, half:]
    row_at = lax.broadcasted_iota(jnp.int32, (n, n), 0)
    col_at = lax.broadcasted_iota(jnp.int32, (n, n), 1)
    gram = work[...]
    diagonal = jnp.where(row_at == col_at, gram, 0.0)
    scale_cols = lax.rsqrt(jnp.sum(diagonal, axis=0, keepdims=True))
    scale_rows = lax.rsqrt(jnp.sum(diagonal, axis=1, keepdims=True))
    work[...] = gram * (scale_rows * scale_cols)

    def step(k, carry):
        first = pl.multiple_of(k * BLOCK, BLOCK)
        here = pl.ds(first, BLOCK)
        block = work[here, here]
        tiles = factor_block([block[PANEL * i : PANEL * (i + 1), :] for i in range(BLOCK // PANEL)])
        ri = lax.broadcasted_iota(jnp.int32, (BLOCK, BLOCK), 0)
        ci = lax.broadcasted_iota(jnp.int32, (BLOCK, BLOCK), 1)
        lower_inverse = jnp.where(ci <= ri, jnp.concatenate(tiles, axis=0), 0.0)
        work[here, here] = jnp.where(ci == ri, 1.0, 0.0)
        work[here, :] = jnp.dot(lower_inverse, work[here, :], precision=HIGHEST, preferred_element_type=F32)
        for at in range(BLOCK, n, BLOCK):

            @pl.when(first + BLOCK == at)
            def _():
                done = slice(at - BLOCK, at)
                work[at:, done] = jnp.zeros((n - at, BLOCK), F32)
                work[at:, :] -= lax.dot_general(
                    work[done, at:],
                    work[done, :],
                    (((0,), (0,)), ((), ())),
                    precision=HIGHEST,
                    preferred_element_type=F32,
                )

        return carry

    lax.fori_loop(0, n // BLOCK, step, 0)
    work[...] = jnp.where(col_at <= row_at, work[...], 0.0) * scale_cols
    for ref in out_ref:
        ref[:, :half] = work[:, own]
        ref[:, half:] = work[:, far]
    for i in range(half // chunk):
        for core, to in ((1 - core_ref[0], i * chunk), (core_ref[0], half + i * chunk)):
            rows = pl.ds(pl.multiple_of((2 * i + core) * chunk, chunk), chunk)
            turned_ref[to : to + chunk, :half] = work[rows, own]
            turned_ref[to : to + chunk, half:] = work[rows, far]


def inverse_factor(core, mine, other, chunk, whole):
    n = mine.shape[1]
    vmem = pl.BlockSpec(memory_space=pltpu.VMEM)
    return pl.pallas_call(
        functools.partial(inverse_factor_kernel, chunk),
        in_specs=[pl.BlockSpec(memory_space=pltpu.SMEM), vmem, vmem],
        out_specs=[vmem] * (1 + whole),
        out_shape=[jax.ShapeDtypeStruct((n, n), F32)] * (1 + whole),
        scratch_shapes=[pltpu.VMEM((n, n), F32)],
        compiler_params=pltpu.CompilerParams(vmem_limit_bytes=16 << 20),
        cost_estimate=pl.CostEstimate(flops=2 * n**3, bytes_accessed=8 * n * n, transcendentals=4 * n),
    )(jnp.full((1,), core, jnp.int32), mine, other)


def product_kernel(transposed, at_ref, left_ref, right_ref, out_ref):
    cols = out_ref.shape[1]
    right = right_ref[...] if transposed else right_ref[:, pl.ds(pl.multiple_of(at_ref[0] * cols, cols), cols)]
    out_ref[...] = lax.dot_general(
        left_ref[...], right, (((1,), (int(transposed),)), ((), ())), preferred_element_type=F32
    )


def product(left, right, cols, at=0, transposed=False):
    rows, depth = left.shape
    tile = min(rows, 256)
    return pl.pallas_call(
        functools.partial(product_kernel, transposed),
        grid=(rows // tile,),
        in_specs=[
            pl.BlockSpec(memory_space=pltpu.SMEM),
            pl.BlockSpec((tile, depth), lambda i: (i, 0)),
            pl.BlockSpec(right.shape, lambda i: (0, 0)),
        ],
        out_specs=pl.BlockSpec((tile, cols), lambda i: (i, 0)),
        out_shape=jax.ShapeDtypeStruct((rows, cols), F32),
        compiler_params=pltpu.CompilerParams(vmem_limit_bytes=16 << 20),
        cost_estimate=pl.CostEstimate(
            flops=2 * rows * cols * depth,
            bytes_accessed=2 * (rows + cols) * depth + 4 * rows * cols,
            transcendentals=0,
        ),
    )(jnp.full((1,), at, jnp.int32), left, right)


def this_core():
    return lax.rem(lax.axis_index("row"), 2)


def pick(array, at):
    return lax.dynamic_index_in_dim(array, lax.rem(at, array.shape[0]), 0, keepdims=False)


def swap_cores(array):
    return lax.ppermute(array, "row", [(i, i ^ 1) for i in range(lax.axis_size("row"))])


def send_col(array, step):
    size = lax.axis_size("col")
    return lax.ppermute(array, "col", [(i, (i + step) % size) for i in range(size)])


def flip_col(array, bits):
    return lax.ppermute(array, "col", [(i, i ^ bits) for i in range(lax.axis_size("col"))])


def exchange(pieces):
    rows = lax.axis_size("row")
    groups = [list(range(core, rows, 2)) for core in range(2)]
    return lax.all_to_all(pieces, "row", 0, 0, tiled=True, axis_index_groups=groups)


def spread(share):
    chips = lax.axis_size("row") // 2
    return exchange(lax.optimization_barrier(jnp.broadcast_to(share[None], (chips,) + share.shape)))


def sum_gram(share):
    chips = lax.axis_size("row") // 2
    n = share.shape[1]
    other = swap_cores(share)
    both = jnp.concatenate([share, jnp.concatenate([other[:, n // 2 :], other[:, : n // 2]], axis=1)])
    half = lax.dot_general(
        both[:, : n // 2], both, (((0,), (0,)), ((), ())), precision=HIGHEST, preferred_element_type=F32
    )
    own = jnp.sum(exchange(half.reshape(chips, n // (2 * chips), n)), axis=0)
    pair = own + flip_col(own, 1)
    total = (pair + flip_col(pair, 2)) + (flip_col(pair, 4) + flip_col(pair, 6))
    mine = spread(total).reshape(n // 2, n)
    return pair, mine, swap_cores(mine)


def sum_cols(partials):
    size = lax.axis_size("col")
    me = lax.axis_index("col")
    far = size // 2
    sums = []
    for at, partial in enumerate(partials):
        blocks = partial.reshape(size, partial.shape[0] // size, partial.shape[1])
        own = pick(blocks, me)
        for way in (1, -1):
            hops = far if (way == 1) == (at == 0) else size - 1 - far
            moving = pick(blocks, me + size + way * hops)
            for left in range(hops - 1, -1, -1):
                moving = send_col(moving, way)
                if left > 0:
                    moving = moving + pick(blocks, me + size + way * left)
            own = own + moving
        sums.append(own)
    return jnp.concatenate(sums, axis=1)


def factor(partials, chunk, whole):
    share = sum_cols(partials)
    pair, mine, other = sum_gram(share)
    share, _ = lax.optimization_barrier((share, pair))
    sampled = lax.all_gather(share, "col", axis=0, tiled=True)
    return sampled, inverse_factor(this_core(), mine, other, chunk, whole)


def times_transposed(sampled, lower_inverse, precision):
    return lax.dot_general(
        sampled,
        lower_inverse,
        (((1,), (1,)), ((), ())),
        precision=precision,
        preferred_element_type=F32,
    )


def project(sampled, turned, activations, precision, beside):
    chips = lax.axis_size("row") // 2
    basis_half = times_transposed(sampled, turned, precision).astype(BF16)
    n = basis_half.shape[1] // 2

    def half(columns):
        return lax.dot_general(
            columns, activations, (((0,), (0,)), ((), ())), preferred_element_type=F32
        )

    arrived = swap_cores(half(basis_half[:, :n]).astype(BF16))
    stay, beside = lax.optimization_barrier((half(basis_half[:, n:]), beside))
    pair = (stay + arrived.astype(F32)).astype(BF16)
    pair, beside = lax.optimization_barrier((pair.reshape(chips, n // chips, pair.shape[1]), beside))
    return jnp.sum(exchange(pair).astype(F32), axis=0), beside


def body(activations, sketch):
    rows_dev, cols_dev = activations.shape
    rank = sketch.shape[1]
    row_count = lax.axis_size("row")
    half = rank // 2
    core = this_core()
    partials = [product(activations, sketch, half, at) for at in (core, 1 - core)]
    sampled, (turned,) = factor(partials, half, False)
    share, _ = project(sampled, turned, activations, HIGHEST, ())
    mine = spread(share.astype(BF16)).reshape(half, cols_dev)
    partials = [product(activations, gathered, half, transposed=True) for gathered in (mine, swap_cores(mine))]
    sampled, (turned, lower_inverse) = factor(partials, rank // row_count, True)
    scaled_basis = math.sqrt(rows_dev * row_count) * times_transposed(sampled, lower_inverse, HIGHEST)
    coefficients, scaled_basis = project(sampled, turned, activations, HIGH, scaled_basis)
    return (scaled_basis, coefficients)


def solution(mesh):
    in_specs = (P("row", "col"), P("col", None))
    out_specs = (P("row", None), P("row", "col"))
    return jax.shard_map(body, mesh=mesh, in_specs=in_specs, out_specs=out_specs, check_vma=False)
```
